256 devices in a mesh: section: 64 (over x, y_hi, z), tp: 4 (over y_lo, core).
Axes of the slice: x: 4, y: 4 (y_hi: 2, y_lo: 2; y = y_hi * 2 + y_lo), z: 8, core: 2. Of those that a mesh axis runs over, the one named last changes fastest.
Arguments:
- hidden: bfloat16 [64, 256, 2, 2048], P('section', 'tp'), may hold values from -6 to 6
- upstream: bfloat16 [64, 256, 2, 2048], P('section', 'tp'), may hold values from -6 to 6
- w_qkv: bfloat16 [64, 3, 2048, 2048], P('section', None, None, 'tp'), may hold values from -0.125 to 0.125
- w_out: bfloat16 [64, 2048, 2048], P('section', 'tp'), may hold values from -0.125 to 0.125
- norm_gain: float32 [64, 2048], P('section'), may hold values from 0.5 to 5, as said below
- final_gain: float32 [2048], replicated, may hold values from 0.5 to 2
Outputs:
- section_out: bfloat16 [64, 256, 2, 2048], P('section', 'tp')
- grad_in: bfloat16 [64, 256, 2, 2048], P('section', 'tp')
- memory_grad_out: bfloat16 [64, 256, 2, 2048], P('section', 'tp')
The draws below stay inside these ranges and needn't reach their ends.
Inputs may be any that keep to these rules, and one draw needn't show every extreme that they name: `norm_gain`: gains of the sections' norms.
All inputs are finite; a program needn't handle non-finite values.
Results may differ from the reference program's by a relative error of at most 0.035.
The reference program's roundings to bfloat16 on the way count: a program that leaves them out, or rounds other values in their place, can miss the bound.
Values may be sent and summed in bfloat16 or wider, within the bound.
No kernel may reach another device: no remote copies, remote signals or barrier semaphores. Data moves between devices by JAX's collectives and lax.ppermute only.
A program may use at most 192 MiB of HBM per device.

```python
import math
import jax
import jax.numpy as jnp
from jax import lax

D = 2048
HEAD_DIM = 256
SEQ = 256
MICRO = 2
INNER = 2048
N_SECTION = 64


def draw_norm_gain(key, part):
    key = jax.random.fold_in(key, 11)
    second_key = jax.random.fold_in(key, 1)
    return jnp.exp(jax.random.uniform(second_key, (N_SECTION, D), jnp.float32, math.log(0.5), math.log(2.0)))


def shard_levels(key, shape, shards, smallest, top_value):
    def one(position, parts):
        heights = jax.random.uniform(jax.random.fold_in(jax.random.fold_in(key, 6), position), (parts,), jnp.float32, smallest / len(shards), top_value / len(shards))
        return jnp.repeat(jnp.exp(heights), shape[position] // parts).reshape((-1,) + (1,) * (len(shape) - position - 1))

    level = one(*shards[0])
    for cut in shards[1:]:
        level = level * one(*cut)
    return level


def normal_values(key, dims, spread, bound, cuts=(), dtype=jnp.bfloat16):
    array = jax.random.normal(key, dims, jnp.float32) * spread
    if len(cuts) > 0:
        array = shard_levels(key, dims, cuts, -0.22, 0.18) * array
    return jnp.clip(array, min=-bound, max=bound).astype(dtype)


def setup_inputs(seed: int = 0) -> dict:
    seeds = jax.random.split(jax.random.key(seed), 7)
    hidden = normal_values(seeds[0], (N_SECTION, SEQ, MICRO, D), 1.0, 6.0, ((0, 64), (1, 4)))
    upstream = normal_values(seeds[1], (N_SECTION, SEQ, MICRO, D), 1.0, 6.0, ((0, 64), (1, 4)))
    w_qkv = normal_values(seeds[2], (N_SECTION, 3, D, INNER), D ** -0.5, 0.125, ((0, 64), (3, 4)))
    w_out = normal_values(seeds[3], (N_SECTION, INNER, D), INNER ** -0.5, 0.125, ((0, 64), (1, 4)))
    norm_gain = draw_norm_gain(jax.random.fold_in(seeds[6], 71), 0)
    final_gain = jnp.clip(jax.random.uniform(seeds[5], (D,), jnp.float32, 0.5, 2.0), 0.5, 2.0)
    return dict(hidden=hidden, upstream=upstream, w_qkv=w_qkv, w_out=w_out, norm_gain=norm_gain, final_gain=final_gain)


epsilon = 1e-06

def normalize(inputs, gain):
    values = inputs.astype(jnp.float32)
    inverse = lax.rsqrt(lax.optimization_barrier(jnp.mean(values * values, axis=-1, keepdims=True)) + epsilon)
    return ((values * inverse * gain).astype(jnp.bfloat16), inverse)

def norm_back(inputs, inverse, d_normed, base):
    values = inputs.astype(jnp.float32)
    inner_mean = lax.optimization_barrier(jnp.mean(values * d_normed, axis=-1, keepdims=True))
    return base.astype(jnp.float32) + inverse * d_normed - values * inverse * inverse * inverse * inner_mean

def split_heads(tensor):
    return tensor.reshape(tensor.shape[0], tensor.shape[1], -1, HEAD_DIM)

def join_heads(tensor):
    return tensor.reshape(tensor.shape[0], tensor.shape[1], -1)

def forward(inputs, weights, w_output, gain, source):
    normed, inverse = normalize(inputs, gain)
    key_input = normed if source is None else source
    query = split_heads(jnp.dot(normed, weights[0], preferred_element_type=jnp.float32).astype(jnp.bfloat16))
    keys = split_heads(jnp.dot(key_input, weights[1], preferred_element_type=jnp.float32).astype(jnp.bfloat16))
    values = split_heads(jnp.dot(key_input, weights[2], preferred_element_type=jnp.float32).astype(jnp.bfloat16))
    score_scale = HEAD_DIM ** (-0.5)
    scores = jnp.einsum('smhe,tmhe->mhst', query.astype(jnp.float32), keys.astype(jnp.float32)) * score_scale
    attention = jax.nn.softmax(scores, axis=-1)
    rounded = attention.astype(jnp.bfloat16)
    mixed = jnp.einsum('mhst,tmhe->smhe', rounded.astype(jnp.float32), values.astype(jnp.float32))
    mixed = join_heads(mixed.astype(jnp.bfloat16))
    result = (inputs.astype(jnp.float32) + jnp.dot(mixed, w_output, preferred_element_type=jnp.float32)).astype(jnp.bfloat16)
    return (result, (inverse, query, keys, values, attention, rounded))

def backward(grad_out, inputs, weights, w_output, gain, saved, cross):
    inverse, query, keys, values, attention, rounded = saved
    score_scale = HEAD_DIM ** (-0.5)
    d_mixed = split_heads(jnp.dot(grad_out, w_output.T, preferred_element_type=jnp.float32).astype(jnp.bfloat16))
    d_rounded = jnp.einsum('smhe,tmhe->mhst', d_mixed.astype(jnp.float32), values.astype(jnp.float32))
    d_values = jnp.einsum('mhst,smhe->tmhe', rounded.astype(jnp.float32), d_mixed.astype(jnp.float32))
    d_values = join_heads(d_values.astype(jnp.bfloat16))
    d_scores = attention * (d_rounded - lax.optimization_barrier(jnp.sum(d_rounded * attention, axis=-1, keepdims=True))) * score_scale
    d_scores = d_scores.astype(jnp.bfloat16).astype(jnp.float32)
    d_query = join_heads(jnp.einsum('mhst,tmhe->smhe', d_scores, keys.astype(jnp.float32)).astype(jnp.bfloat16))
    d_keys = join_heads(jnp.einsum('mhst,smhe->tmhe', d_scores, query.astype(jnp.float32)).astype(jnp.bfloat16))
    d_normed = jnp.dot(d_query, weights[0].T, preferred_element_type=jnp.float32)
    d_source = jnp.dot(d_keys, weights[1].T, preferred_element_type=jnp.float32)
    d_source = d_source + jnp.dot(d_values, weights[2].T, preferred_element_type=jnp.float32)
    if not cross:
        d_normed = d_normed + d_source
    grad_input = norm_back(inputs, inverse, d_normed * gain, grad_out).astype(jnp.bfloat16)
    return (grad_input, d_source)

def reference(hidden, upstream, w_qkv, w_out, norm_gain, final_gain):
    enc_sections = N_SECTION // 2

    def enc_step(section_items):
        inputs, grad_out, weights, w_output, gain = section_items
        result, saved = forward(inputs, weights, w_output, gain, None)
        grad_input = backward(grad_out, inputs, weights, w_output, gain, saved, False)[0]
        return (result, grad_input)
    enc_out, enc_grad = lax.map(enc_step, (hidden[:enc_sections], upstream[:enc_sections], w_qkv[:enc_sections], w_out[:enc_sections], norm_gain[:enc_sections]))
    enc_last = enc_out[enc_sections - 1]
    memory, last_inverse = normalize(enc_last, final_gain)

    def dec_step(running, section_items):
        inputs, grad_out, weights, w_output, gain = section_items
        result, saved = forward(inputs, weights, w_output, gain, memory)
        grad_input, d_source = backward(grad_out, inputs, weights, w_output, gain, saved, True)
        return (running + d_source, (result, grad_input))
    memory_grad, (dec_out, dec_grad) = lax.scan(dec_step, jnp.zeros(enc_last.shape, jnp.float32), (hidden[enc_sections:], upstream[enc_sections:], w_qkv[enc_sections:], w_out[enc_sections:], norm_gain[enc_sections:]))
    memory_grad_out = norm_back(enc_last, last_inverse, memory_grad * final_gain, jnp.zeros(enc_last.shape, jnp.float32))
    memory_grad_out = memory_grad_out.astype(jnp.bfloat16)
    memory_copies = jnp.broadcast_to(memory_grad_out[None], (N_SECTION,) + memory_grad_out.shape)
    section_out = jnp.concatenate([enc_out, dec_out], axis=0)
    grad_in = jnp.concatenate([enc_grad, dec_grad], axis=0)
    return (section_out, grad_in, memory_copies)
```

```python
import jax
import jax.numpy as jnp
from jax import lax
from jax.sharding import PartitionSpec as P

HEAD_DIM = 256
epsilon = 1e-06

NX, NY, NZ = 4, 2, 8
CORE_SWAP = [(t, t ^ 1) for t in range(4)]
CHIP_SWAP = [(t, t ^ 2) for t in range(4)]


def sec(x, y, z):
    return (x * NY + y) * NZ + z


def x_perm(k, sources):
    return [(sec(x, y, z), sec(x ^ k, y, z)) for x in sources for y in range(NY) for z in range(NZ)]


Y_SWAP = [(sec(x, y, z), sec(x, y ^ 1, z)) for x in range(NX) for y in range(NY) for z in range(NZ)]


def z_swap(k):
    return [(sec(x, y, z), sec(x, y, z ^ k)) for x in range(NX) for y in range(NY) for z in range(NZ)]


def z_from(pairs):
    return [(sec(x, y, a), sec(x, y, b)) for x in (2, 3) for y in range(NY) for a, b in pairs]


def dot(a, b):
    return jnp.dot(a, b, preferred_element_type=jnp.float32)


def dot_t(a, b):
    return lax.dot_general(a, b, (((1,), (1,)), ((), ())), preferred_element_type=jnp.float32)


def t_dot(a, b):
    return lax.dot_general(a, b, (((0,), (0,)), ((), ())), preferred_element_type=jnp.float32)


def normalize(inputs, gain):
    values = inputs.astype(jnp.float32)
    inverse = lax.rsqrt(jnp.mean(values * values, axis=-1, keepdims=True) + epsilon)
    return ((values * inverse * gain).astype(jnp.bfloat16), inverse)


def norm_back(inputs, inverse, d_normed, base):
    values = inputs.astype(jnp.float32)
    inner_mean = jnp.mean(values * d_normed, axis=-1, keepdims=True)
    return base + inverse * d_normed - values * inverse * inverse * inverse * inner_mean


def gather_rows(rows):
    other = lax.ppermute(rows, "tp", CHIP_SWAP)
    half = jnp.concatenate([rows, other], axis=0)
    return jnp.concatenate([half, lax.ppermute(half, "tp", CORE_SWAP)], axis=0)


def scatter_sum(partial):
    count = partial.shape[0] // 4
    got = lax.ppermute(partial[2 * count :].astype(jnp.bfloat16), "tp", CORE_SWAP)
    kept = partial[: 2 * count] + got.astype(jnp.float32)
    got = lax.ppermute(kept[count:].astype(jnp.bfloat16), "tp", CHIP_SWAP)
    return kept[:count] + got.astype(jnp.float32)


def spread(rows):
    root = sec(1, 1, 7)
    held = lax.ppermute(rows, "section", [(root, sec(2, 1, 7))]) + lax.ppermute(
        rows, "section", [(root, sec(3, 1, 7))]
    )
    held = held + lax.ppermute(held, "section", [(sec(x, 1, 7), sec(x, 0, 7)) for x in (2, 3)])
    held = (
        held
        + lax.ppermute(held, "section", z_from([(7, 3)]))
        + lax.ppermute(held, "section", z_from([(7, 0)]))
        + lax.ppermute(held, "section", z_from([(7, 6)]))
    )
    return (
        held
        + lax.ppermute(held, "section", z_from([(3, 4), (0, 1), (6, 5)]))
        + lax.ppermute(held, "section", z_from([(3, 2)]))
    )


def local(hidden, upstream, w_qkv, w_out, norm_gain, final_gain):
    micros = range(hidden.shape[2])
    rows = hidden.shape[1]
    weights = w_qkv[0]
    w_output = w_out[0]
    gain = norm_gain[0]
    head_count = weights.shape[2] // HEAD_DIM
    scale = HEAD_DIM ** (-0.5)
    section_id = lax.axis_index("section")
    x_id = section_id // (NY * NZ)
    y_id = (section_id // NZ) % NY
    is_decoder = x_id >= NX // 2

    def heads_of(tensor):
        return [tensor[:, h * HEAD_DIM : (h + 1) * HEAD_DIM] for h in range(head_count)]

    def attend(query, keys, values):
        out = []
        for q, k, v in zip(heads_of(query), heads_of(keys), heads_of(values)):
            attention = jax.nn.softmax(dot_t(q, k) * scale, axis=-1)
            rounded = attention.astype(jnp.bfloat16)
            out.append((attention, rounded, dot(rounded, v).astype(jnp.bfloat16)))
        return out

    def project_out(attended):
        return dot(jnp.concatenate([a[2] for a in attended], axis=1), w_output)

    inputs = [hidden[0, :, m] for m in micros]
    grads = [upstream[0, :, m] for m in micros]

    norms = [normalize(v, gain) for v in inputs]
    query, own_keys, own_values, enc_out = [], [], [], []
    for m in micros:
        normed = gather_rows(norms[m][0])
        query.append(dot(normed, weights[0]).astype(jnp.bfloat16))
        own_keys.append(dot(normed, weights[1]).astype(jnp.bfloat16))
        own_values.append(dot(normed, weights[2]).astype(jnp.bfloat16))
        attended = attend(query[m], own_keys[m], own_values[m])
        summed = scatter_sum(project_out(attended))
        enc_out.append((inputs[m].astype(jnp.float32) + summed).astype(jnp.bfloat16))
    enc_last = [spread(v) for v in enc_out]

    d_mixed = [dot_t(gather_rows(g), w_output).astype(jnp.bfloat16) for g in grads]

    section_out, grad_in, sources = [], [], []
    for m in micros:
        memory = gather_rows(normalize(enc_last[m], final_gain)[0])
        keys = jnp.where(is_decoder, dot(memory, weights[1]).astype(jnp.bfloat16), own_keys[m])
        values = jnp.where(is_decoder, dot(memory, weights[2]).astype(jnp.bfloat16), own_values[m])
        attended = attend(query[m], keys, values)
        d_query, d_keys, d_values = [], [], []
        for (attention, rounded, _), q, k, v, dm in zip(
            attended, heads_of(query[m]), heads_of(keys), heads_of(values), heads_of(d_mixed[m])
        ):
            d_rounded = dot_t(dm, v)
            d_values.append(t_dot(rounded, dm).astype(jnp.bfloat16))
            d_scores = attention * (
                d_rounded - jnp.sum(d_rounded * attention, axis=-1, keepdims=True)
            )
            d_scores = (d_scores * scale).astype(jnp.bfloat16)
            d_query.append(dot(d_scores, k).astype(jnp.bfloat16))
            d_keys.append(t_dot(d_scores, q).astype(jnp.bfloat16))
        d_query, d_keys, d_values = (
            jnp.concatenate(v, axis=1) for v in (d_query, d_keys, d_values)
        )
        source = dot_t(d_keys, weights[1]) + dot_t(d_values, weights[2])
        sources.append(jnp.where(is_decoder, scatter_sum(source), 0.0))
        d_normed = dot_t(d_query, weights[0]) + jnp.where(is_decoder, 0.0, source)
        d_normed = scatter_sum(d_normed)
        grad_in.append(
            norm_back(
                inputs[m], norms[m][1], d_normed * gain, grads[m].astype(jnp.float32)
            ).astype(jnp.bfloat16)
        )
        summed = scatter_sum(project_out(attended))
        section_out.append((inputs[m].astype(jnp.float32) + summed).astype(jnp.bfloat16))

    quarter, eighth = rows // NX, rows // (NX * NY)

    def quarter_of(v, x):
        return lax.dynamic_slice_in_dim(v, x * quarter, quarter, axis=0)

    def eighth_of(v, y):
        return lax.dynamic_slice_in_dim(v, y * eighth, eighth, axis=0)

    memory_grad_out = []
    for m in micros:
        last = quarter_of(enc_last[m], x_id)
        last = last + lax.ppermute(quarter_of(enc_last[m], x_id ^ 3), "section", x_perm(3, (2, 3)))
        last = eighth_of(last, y_id)
        total = quarter_of(sources[m], x_id)
        wire = sources[m].astype(jnp.bfloat16)
        for k in (1, 2, 3):
            got = lax.ppermute(quarter_of(wire, x_id ^ k), "section", x_perm(k, (2, 3)))
            total = total + got.astype(jnp.float32)
        got = lax.ppermute(eighth_of(total, y_id ^ 1).astype(jnp.bfloat16), "section", Y_SWAP)
        total = eighth_of(total, y_id) + got.astype(jnp.float32)
        for k in (4, 2, 1):
            wire = total.astype(jnp.bfloat16)
            got = lax.ppermute(wire, "section", z_swap(k))
            total = wire.astype(jnp.float32) + got.astype(jnp.float32)
        inverse = normalize(last, final_gain)[1]
        out = norm_back(last, inverse, total * final_gain, 0.0).astype(jnp.bfloat16)
        got = lax.ppermute(out, "section", Y_SWAP)
        out = jnp.where(
            y_id == 0,
            jnp.concatenate([out, got], axis=0),
            jnp.concatenate([got, out], axis=0),
        )
        parts = [out] + [lax.ppermute(out, "section", x_perm(k, range(NX))) for k in (1, 2, 3)]
        odd, high = (x_id & 1) == 1, (x_id & 2) == 2
        parts = [jnp.where(odd, parts[j ^ 1], parts[j]) for j in range(4)]
        parts = [jnp.where(high, parts[j ^ 2], parts[j]) for j in range(4)]
        memory_grad_out.append(jnp.concatenate(parts, axis=0))

    return tuple(
        jnp.stack(v, axis=1)[None] for v in (section_out, grad_in, memory_grad_out)
    )


def solution(mesh):
    in_specs = (
        P("section", "tp", None, None),
        P("section", "tp", None, None),
        P("section", None, None, "tp"),
        P("section", "tp", None),
        P("section", None),
        P(),
    )
    out_specs = (
        P("section", "tp", None, None),
        P("section", "tp", None, None),
        P("section", "tp", None, None),
    )
    return jax.shard_map(local, mesh=mesh, in_specs=in_specs, out_specs=out_specs, check_vma=False)
```

```python
import jax
import jax.numpy as jnp
from jax import lax
from jax.experimental import pallas as pl
from jax.experimental.pallas import tpu as pltpu
from jax.sharding import PartitionSpec as P

HEAD_DIM = 256
epsilon = 1e-06

NX, NY, NZ = 4, 2, 8
CORE_SWAP = [(t, t ^ 1) for t in range(4)]
CHIP_SWAP = [(t, t ^ 2) for t in range(4)]


def sec(x, y, z):
    return (x * NY + y) * NZ + z


def x_perm(k, sources):
    return [(sec(x, y, z), sec(x ^ k, y, z)) for x in sources for y in range(NY) for z in range(NZ)]


Y_SWAP = [(sec(x, y, z), sec(x, y ^ 1, z)) for x in range(NX) for y in range(NY) for z in range(NZ)]


def z_swap(k):
    return [(sec(x, y, z), sec(x, y, z ^ k)) for x in range(NX) for y in range(NY) for z in range(NZ)]


def dot(a, b):
    return jnp.dot(a, b, preferred_element_type=jnp.float32)


def dot_t(a, b):
    return lax.dot_general(a, b, (((1,), (1,)), ((), ())), preferred_element_type=jnp.float32)


def t_dot(a, b):
    return lax.dot_general(a, b, (((0,), (0,)), ((), ())), preferred_element_type=jnp.float32)


def normalize(inputs, gain):
    values = inputs.astype(jnp.float32)
    inverse = lax.rsqrt(jnp.mean(values * values, axis=-1, keepdims=True) + epsilon)
    return ((values * inverse * gain).astype(jnp.bfloat16), inverse)


def norm_back(inputs, inverse, d_normed, base):
    values = inputs.astype(jnp.float32)
    inner_mean = jnp.mean(values * d_normed, axis=-1, keepdims=True)
    return base + inverse * d_normed - values * inverse * inverse * inverse * inner_mean


def chip_swap(rows):
    return lax.ppermute(rows, "tp", CHIP_SWAP)


def core_swap(rows):
    return lax.ppermute(rows, "tp", CORE_SWAP)


def gather_rows(rows):
    other = chip_swap(rows)
    return jnp.concatenate([rows, other, core_swap(rows), core_swap(other)], axis=0)


def halves(rows):
    count = rows.shape[0] // 2
    return rows[:count], rows[count:]


def sum_cores(kept, sent):
    kept, sent = halves(kept + core_swap(sent.astype(jnp.bfloat16)).astype(jnp.float32))
    return kept, sent.astype(jnp.bfloat16)


def sum_chips(kept, sent):
    return kept + chip_swap(sent).astype(jnp.float32)


def scatter_sum(kept, sent):
    return sum_chips(*sum_cores(kept, sent))


def together(*values):
    return lax.optimization_barrier(values)


def move(rows, pairs):
    return lax.ppermute(rows, "section", pairs)


def ordered(mine, got, first):
    return jnp.where(
        first, jnp.concatenate([mine, got], axis=0), jnp.concatenate([got, mine], axis=0)
    )


def spread(rows, x_id, y_id, z_id):
    def pairs(*hops):
        return [(sec(x, y, a), sec(x, y, b)) for x in (2, 3) for y in range(NY) for a, b in hops]

    count = rows.shape[0] // 4
    held = None
    for index in (2, 0, 3, 1):
        x, y = 2 + index // 2, index % 2
        piece = rows[index * count : (index + 1) * count]
        got = move(piece, [(sec(1, 1, 7), sec(x, y, 7))])
        held = got if held is None else jnp.where((x_id == x) & (y_id == y), got, held)
    five = move(held, pairs((7, 5)))
    one = move(held, pairs((7, 1)))
    held = jnp.where(z_id == 5, five, jnp.where(z_id == 1, one, held))
    far = move(held, pairs((1, 3), (5, 4)))
    near = move(held, pairs((7, 0), (1, 2), (5, 6)))
    from_far = (z_id == 3) | (z_id == 4)
    from_near = (z_id == 0) | (z_id == 2) | (z_id == 6)
    held = jnp.where(from_far, far, jnp.where(from_near, near, held))
    held = ordered(held, move(held, Y_SWAP), y_id == 0)
    return ordered(held, move(held, x_perm(1, (2, 3))), x_id == 2)


SCALE = HEAD_DIM ** (-0.5)
TILE = 512


def head_slices(width):
    return [slice(h * HEAD_DIM, (h + 1) * HEAD_DIM) for h in range(width // HEAD_DIM)]


def softmax(q, k):
    scores = dot_t(q, k) * SCALE
    raised = jnp.exp(scores - jnp.max(scores, axis=-1, keepdims=True))
    return raised / jnp.sum(raised, axis=-1, keepdims=True)


def fill(pieces, rows_ref):
    count = rows_ref.shape[0] // len(pieces)
    for i, piece in enumerate(pieces):
        rows_ref[i * count : (i + 1) * count, :] = piece[...]


def load(pairs, sems):
    copies = [pltpu.make_async_copy(a, b, sems.at[i]) for i, (a, b) in enumerate(pairs)]
    for copy in copies:
        copy.start()
    return copies


def tiles_of(width):
    return [slice(t, t + TILE) for t in range(0, width, TILE)]


def forward_kernel(p0, p1, p2, p3, w_ref, o_ref, q_ref, k_ref, v_ref, kept_ref, sent_ref,
                   rows_ref, w_buf, o_buf, mixed_ref, sems):
    copies = load([(w_ref.at[0, i], w_buf.at[i]) for i in range(3)] + [(o_ref.at[0], o_buf)], sems)
    fill((p0, p1, p2, p3), rows_ref)
    for i, out in enumerate((q_ref, k_ref, v_ref)):
        copies[i].wait()
        for cols in tiles_of(out.shape[1]):
            out[:, cols] = dot(rows_ref[...], w_buf[i, :, cols]).astype(jnp.bfloat16)
    for cols in head_slices(q_ref.shape[1]):
        rounded = softmax(q_ref[:, cols], k_ref[:, cols]).astype(jnp.bfloat16)
        mixed_ref[:, cols] = dot(rounded, v_ref[:, cols]).astype(jnp.bfloat16)
    copies[3].wait()
    half = kept_ref.shape[0]
    for cols in tiles_of(o_buf.shape[1]):
        part = dot(mixed_ref[...], o_buf[:, cols])
        kept_ref[:, cols] = part[:half]
        sent_ref[:, cols] = part[half:].astype(jnp.bfloat16)


def backward_kernel(dec_ref, p0, p1, p2, p3, w_ref, q_ref, own_k, own_v, dm_ref,
                    k_ref, mixed_ref, ds_ref, kept_ref, sent_ref,
                    rows_ref, w_buf, v_ref, dk_ref, dv_ref, sems):
    copies = load([(w_ref.at[0, i + 1], w_buf.at[i]) for i in range(2)], sems)
    fill((p0, p1, p2, p3), rows_ref)
    decoder = dec_ref[0] == 1
    for i, (out, own) in enumerate(((k_ref, own_k), (v_ref, own_v))):
        copies[i].wait()
        for cols in tiles_of(out.shape[1]):
            made = dot(rows_ref[...], w_buf[i, :, cols]).astype(jnp.bfloat16)
            out[:, cols] = jnp.where(decoder, made, own[:, cols])
    for cols in head_slices(q_ref.shape[1]):
        q, k, v, dm = q_ref[:, cols], k_ref[:, cols], v_ref[:, cols], dm_ref[:, cols]
        attention = softmax(q, k)
        rounded = attention.astype(jnp.bfloat16)
        mixed_ref[:, cols] = dot(rounded, v).astype(jnp.bfloat16)
        d_rounded = dot_t(dm, v)
        dv_ref[:, cols] = t_dot(rounded, dm).astype(jnp.bfloat16)
        d_scores = attention * (d_rounded - jnp.sum(d_rounded * attention, axis=-1, keepdims=True))
        d_scores = (d_scores * SCALE).astype(jnp.bfloat16)
        ds_ref[:, cols] = d_scores
        dk_ref[:, cols] = t_dot(d_scores, q).astype(jnp.bfloat16)
    half = kept_ref.shape[0]
    for cols in tiles_of(kept_ref.shape[1]):
        part = dot_t(dk_ref[...], w_buf[0, cols, :]) + dot_t(dv_ref[...], w_buf[1, cols, :])
        kept_ref[:, cols] = part[:half]
        sent_ref[:, cols] = part[half:].astype(jnp.bfloat16)


def rest_kernel(dec_ref, k_ref, mixed_ref, ds_ref, w_ref, o_ref, src_kept, src_sent,
                kept_ref, sent_ref, out_kept, out_sent, w_buf, o_buf, dq_ref, sems):
    copies = load([(w_ref.at[0, 0], w_buf), (o_ref.at[0], o_buf)], sems)
    for cols in head_slices(k_ref.shape[1]):
        dq_ref[:, cols] = dot(ds_ref[:, cols], k_ref[:, cols]).astype(jnp.bfloat16)
    encoder = dec_ref[0] == 0
    half = kept_ref.shape[0]
    copies[0].wait()
    for cols in tiles_of(kept_ref.shape[1]):
        part = dot_t(dq_ref[...], w_buf[cols, :])
        own = jnp.where(encoder, src_kept[:, cols], 0.0)
        kept_ref[:, cols] = part[:half] + own
        own = jnp.where(encoder, src_sent[:, cols].astype(jnp.float32), 0.0)
        sent_ref[:, cols] = (part[half:] + own).astype(jnp.bfloat16)
    copies[1].wait()
    for cols in tiles_of(kept_ref.shape[1]):
        part = dot(mixed_ref[...], o_buf[:, cols])
        out_kept[:, cols] = part[:half]
        out_sent[:, cols] = part[half:].astype(jnp.bfloat16)


def call(kernel, name, args, outs, scratch, gflop):
    spec = {"v": pl.BlockSpec(memory_space=pltpu.VMEM), "a": pl.BlockSpec(memory_space=pl.ANY)}
    spec["s"] = pl.BlockSpec(memory_space=pltpu.SMEM)
    return pl.pallas_call(
        kernel,
        name=name,
        out_shape=[jax.ShapeDtypeStruct(shape, dtype) for shape, dtype in outs],
        in_specs=[spec[kind] for kind, _ in args],
        out_specs=[spec["v"]] * len(outs),
        scratch_shapes=scratch,
        compiler_params=pltpu.CompilerParams(vmem_limit_bytes=32 * 2**20),
        cost_estimate=pl.CostEstimate(
            flops=int(gflop * 6e9), bytes_accessed=2**20, transcendentals=2**17
        ),
    )(*[value for _, value in args])


def local(hidden, upstream, w_qkv, w_out, norm_gain, final_gain):
    micros = range(hidden.shape[2])
    rows = hidden.shape[1]
    gain = norm_gain[0]
    section_id = lax.axis_index("section")
    x_id = section_id // (NY * NZ)
    y_id = (section_id // NZ) % NY
    z_id = section_id % NZ
    is_decoder = x_id >= NX // 2
    decoder = is_decoder.astype(jnp.int32).reshape(1)

    bf16, f32 = jnp.bfloat16, jnp.float32
    width, inner = hidden.shape[3], w_qkv.shape[3]
    all_rows = 4 * rows
    whole, narrow = (all_rows, width), (all_rows, inner)
    half = (all_rows // 2, width)
    pair = [(half, f32), (half, bf16)]

    inputs = [hidden[0, :, m] for m in micros]
    grads = [upstream[0, :, m] for m in micros]

    def begin_gather(values):
        others, mates = [chip_swap(values[0])], [core_swap(values[0])]
        mates[0], later = together(mates[0], values[1])
        others.append(chip_swap(later))
        mates.append(core_swap(later))
        return others, mates

    norms = [normalize(v, gain) for v in inputs]
    others, mates = begin_gather([n[0] for n in norms])
    projections, projected = [], []
    for m in micros:
        *made, kept, sent = call(
            forward_kernel,
            "forward",
            [("v", v) for v in (norms[m][0], others[m], mates[m], core_swap(others[m]))]
            + [("a", w_qkv), ("a", w_out)],
            [(narrow, bf16)] * 3 + pair,
            [
                pltpu.VMEM(whole, bf16),
                pltpu.VMEM(w_qkv.shape[1:], bf16),
                pltpu.VMEM(w_out.shape[1:], bf16),
                pltpu.VMEM(narrow, bf16),
                pltpu.SemaphoreType.DMA((4,)),
            ],
            2.3,
        )
        if m == 0:
            kept, sent, others[1] = together(kept, sent, others[1])
        projections.append(made)
        projected.append((kept, sent))
    enc_out = [
        (v.astype(jnp.float32) + scatter_sum(*p)).astype(jnp.bfloat16)
        for v, p in zip(inputs, projected)
    ]
    enc_out, grads = together(jnp.concatenate(enc_out, axis=1), grads)
    enc_last = spread(enc_out, x_id, y_id, z_id)
    grad_others = [chip_swap(g) for g in grads]
    enc_last, grad_others = together(enc_last, grad_others)

    memories = [
        normalize(enc_last[:, m * width : (m + 1) * width], final_gain)[0] for m in micros
    ]
    others, mates = begin_gather(memories)
    d_mixed = []
    for g, o in zip(grads, grad_others):
        whole_grad = jnp.concatenate([g, o, core_swap(g), core_swap(o)], axis=0)
        d_mixed.append(dot_t(whole_grad, w_out[0]).astype(bf16))
    partials, saved = [], []
    for m in micros:
        query, own_keys, own_values = projections[m]
        keys, mixed, d_scores, kept, sent = call(
            backward_kernel,
            "backward",
            [("s", decoder)]
            + [("v", v) for v in (memories[m], others[m], mates[m], core_swap(others[m]))]
            + [("a", w_qkv)]
            + [("v", v) for v in (query, own_keys, own_values, d_mixed[m])],
            [(narrow, bf16)] * 3 + pair,
            [
                pltpu.VMEM(whole, bf16),
                pltpu.VMEM((2,) + w_qkv.shape[2:], bf16),
                pltpu.VMEM(narrow, bf16),
                pltpu.VMEM(narrow, bf16),
                pltpu.VMEM(narrow, bf16),
                pltpu.SemaphoreType.DMA((2,)),
            ],
            2.5,
        )
        rest = (keys, mixed, d_scores)
        if m == 0:
            kept, sent, others[1] = together(kept, sent, others[1])
        else:
            kept, sent, rest, saved[0] = together(kept, sent, rest, saved[0])
        partials.append((kept, sent))
        saved.append(rest)

    rests = []
    for m in micros:
        made = call(
            rest_kernel,
            "rest",
            [("s", decoder)]
            + [("v", v) for v in saved[m]]
            + [("a", w_qkv), ("a", w_out)]
            + [("v", v) for v in partials[m]],
            pair * 2,
            [
                pltpu.VMEM(w_qkv.shape[2:], bf16),
                pltpu.VMEM(w_out.shape[1:], bf16),
                pltpu.VMEM(narrow, bf16),
                pltpu.SemaphoreType.DMA((2,)),
            ],
            1.2,
        )
        rests += [sum_cores(*made[:2]), sum_cores(*made[2:])]
    total = jnp.concatenate([scatter_sum(*p) for p in partials], axis=1)
    total, rests = together(jnp.where(is_decoder, total, 0.0), rests)
    rests = [sum_chips(*v) for v in rests]

    quarter, eighth = rows // NX, rows // (NX * NY)

    def quarter_of(v, x):
        return lax.dynamic_slice_in_dim(v, x * quarter, quarter, axis=0)

    def eighth_of(v, y):
        return lax.dynamic_slice_in_dim(v, y * eighth, eighth, axis=0)

    got = move(quarter_of(enc_last, x_id ^ 3), x_perm(3, (2, 3)))
    last = eighth_of(jnp.where(is_decoder, quarter_of(enc_last, x_id), got), y_id)
    last = [last[:, : last.shape[1] // 2], last[:, last.shape[1] // 2 :]]
    wire = total.astype(jnp.bfloat16)
    total = quarter_of(total, x_id)
    for k in (1, 2, 3):
        got = move(quarter_of(wire, x_id ^ k), x_perm(k, (2, 3)))
        total = total + got.astype(jnp.float32)
    got = move(eighth_of(total, y_id ^ 1).astype(jnp.bfloat16), Y_SWAP)
    total = eighth_of(total, y_id) + got.astype(jnp.float32)
    for i, k in enumerate((4, 2, 1)):
        total, rests[i] = together(total, rests[i])
        wire = total.astype(jnp.bfloat16)
        total = wire.astype(jnp.float32) + move(wire, z_swap(k)).astype(jnp.float32)
    total, rests[3] = together(total, rests[3])
    section_out, grad_in = [], []
    for m in micros:
        d_normed, summed = rests[2 * m], rests[2 * m + 1]
        base = grads[m].astype(jnp.float32)
        base = norm_back(inputs[m], norms[m][1], d_normed * gain, base)
        grad_in.append(base.astype(jnp.bfloat16))
        section_out.append((inputs[m].astype(jnp.float32) + summed).astype(jnp.bfloat16))
    total = [total[:, : total.shape[1] // 2], total[:, total.shape[1] // 2 :]]
    out = []
    for m in micros:
        inverse = normalize(last[m], final_gain)[1]
        out.append(norm_back(last[m], inverse, total[m] * final_gain, 0.0).astype(jnp.bfloat16))
    out = jnp.concatenate(out, axis=1)
    got = move(out, Y_SWAP)
    out = jnp.where(
        y_id == 0, jnp.concatenate([out, got], axis=0), jnp.concatenate([got, out], axis=0)
    )
    parts = [out] + [move(out, x_perm(k, range(NX))) for k in (1, 2, 3)]
    odd, high = (x_id & 1) == 1, (x_id & 2) == 2
    parts = [jnp.where(odd, parts[j ^ 1], parts[j]) for j in range(NX)]
    parts = [jnp.where(high, parts[j ^ 2], parts[j]) for j in range(NX)]
    out = jnp.concatenate(parts, axis=0)
    memory_grad_out = [out[:, : out.shape[1] // 2], out[:, out.shape[1] // 2 :]]

    return tuple(
        jnp.stack(v, axis=1)[None] for v in (section_out, grad_in, memory_grad_out)
    )


def solution(mesh):
    in_specs = (
        P("section", "tp", None, None),
        P("section", "tp", None, None),
        P("section", None, None, "tp"),
        P("section", "tp", None),
        P("section", None),
        P(),
    )
    out_specs = (
        P("section", "tp", None, None),
        P("section", "tp", None, None),
        P("section", "tp", None, None),
    )
    return jax.shard_map(local, mesh=mesh, in_specs=in_specs, out_specs=out_specs, check_vma=False)
```

```python
import jax
import jax.numpy as jnp
from jax import lax
from jax.experimental import pallas as pl
from jax.experimental.pallas import tpu as pltpu
from jax.sharding import PartitionSpec as P

HEAD_DIM = 256
epsilon = 1e-06

NX, NY, NZ = 4, 2, 8
CORE_SWAP = [(t, t ^ 1) for t in range(4)]
CHIP_SWAP = [(t, t ^ 2) for t in range(4)]


def sec(x, y, z):
    return (x * NY + y) * NZ + z


def x_perm(k, sources):
    return [(sec(x, y, z), sec(x ^ k, y, z)) for x in sources for y in range(NY) for z in range(NZ)]


def across(pairs):
    def index(x, y, z, low, core):
        return 4 * sec(x, y, z) + 2 * low + core

    return [
        (index(x, a[0], z, a[1], core), index(x, b[0], z, b[1], core))
        for a, b in pairs
        for x in range(NX)
        for z in range(NZ)
        for core in range(2)
    ]


Y_NEXT = across([((y, low), (1 - y, 1 - low)) for y in range(2) for low in range(2)])
Y_BACK = across(
    [((1, low), (0, low)) for low in range(2)] + [((0, low), (1, 1 - low)) for low in range(2)]
)
Y_PAIR = across([((0, low), (0, 1 - low)) for low in range(2)])


def jump(rows, pairs):
    return lax.ppermute(rows, ("section", "tp"), pairs)


def z_swap(k):
    return [(sec(x, y, z), sec(x, y, z ^ k)) for x in range(NX) for y in range(NY) for z in range(NZ)]


def dot(a, b):
    return jnp.dot(a, b, preferred_element_type=jnp.float32)


def dot_t(a, b):
    return lax.dot_general(a, b, (((1,), (1,)), ((), ())), preferred_element_type=jnp.float32)


def t_dot(a, b):
    return lax.dot_general(a, b, (((0,), (0,)), ((), ())), preferred_element_type=jnp.float32)


def normalize(inputs, gain):
    values = inputs.astype(jnp.float32)
    inverse = lax.rsqrt(jnp.mean(values * values, axis=-1, keepdims=True) + epsilon)
    return ((values * inverse * gain).astype(jnp.bfloat16), inverse)


def norm_back(inputs, inverse, d_normed, base):
    values = inputs.astype(jnp.float32)
    inner_mean = jnp.mean(values * d_normed, axis=-1, keepdims=True)
    return base + inverse * d_normed - values * inverse * inverse * inverse * inner_mean


def chip_swap(rows):
    return lax.ppermute(rows, "tp", CHIP_SWAP)


def core_swap(rows):
    return lax.ppermute(rows, "tp", CORE_SWAP)


def gather_rows(rows):
    other = chip_swap(rows)
    return jnp.concatenate([rows, other, core_swap(rows), core_swap(other)], axis=0)


def halves(rows):
    count = rows.shape[0] // 2
    return rows[:count], rows[count:]


def sum_cores(kept, sent):
    kept, sent = halves(kept + core_swap(sent.astype(jnp.bfloat16)).astype(jnp.float32))
    return kept, sent.astype(jnp.bfloat16)


def sum_chips(kept, sent):
    return kept + chip_swap(sent).astype(jnp.float32)


def scatter_sum(kept, sent):
    return sum_chips(*sum_cores(kept, sent))


def together(*values):
    return lax.optimization_barrier(values)


def move(rows, pairs):
    return lax.ppermute(rows, "section", pairs)


def ordered(mine, got, first):
    return jnp.where(
        first, jnp.concatenate([mine, got], axis=0), jnp.concatenate([got, mine], axis=0)
    )


def spread_pieces(rows, x_id, y_id):
    count = rows.shape[0] // 4
    held = None
    for index in (2, 0, 3, 1):
        x, y = 2 + index // 2, index % 2
        piece = rows[index * count : (index + 1) * count]
        root, target = 4 * sec(1, 1, 7), 4 * sec(x, y, 7)
        got = jump(piece, [(root + t, target + (t if y else t ^ 2)) for t in range(4)])
        held = got if held is None else jnp.where((x_id == x) & (y_id == y), got, held)
    return held


def spread_levels(held, z_id):
    def pairs(*hops):
        return [(sec(x, y, a), sec(x, y, b)) for x in (2, 3) for y in range(NY) for a, b in hops]

    five = move(held, pairs((7, 5)))
    one = move(held, pairs((7, 1)))
    held = jnp.where(z_id == 5, five, jnp.where(z_id == 1, one, held))
    far = move(held, pairs((1, 3), (5, 4)))
    near = move(held, pairs((7, 0), (1, 2), (5, 6)))
    from_far = (z_id == 3) | (z_id == 4)
    from_near = (z_id == 0) | (z_id == 2) | (z_id == 6)
    held = jnp.where(from_far, far, jnp.where(from_near, near, held))
    return held


def spread_columns(held, x_id, y_id):
    held = ordered(held, jump(held, Y_NEXT), y_id == 0)
    return ordered(held, move(held, x_perm(1, (2, 3))), x_id == 2)


SCALE = HEAD_DIM ** (-0.5)
TILE = 512


def head_slices(width):
    return [slice(h * HEAD_DIM, (h + 1) * HEAD_DIM) for h in range(width // HEAD_DIM)]


def softmax(q, k):
    scores = dot_t(q, k) * SCALE
    raised = jnp.exp(scores - jnp.max(scores, axis=-1, keepdims=True))
    return raised / jnp.sum(raised, axis=-1, keepdims=True)


def fill(pieces, rows_ref):
    count = rows_ref.shape[0] // len(pieces)
    for i, piece in enumerate(pieces):
        rows_ref[i * count : (i + 1) * count, :] = piece[...]


def load(pairs, sems):
    copies = [pltpu.make_async_copy(a, b, sems.at[i]) for i, (a, b) in enumerate(pairs)]
    for copy in copies:
        copy.start()
    return copies


def tiles_of(width):
    return [slice(t, t + TILE) for t in range(0, width, TILE)]


def forward_kernel(p0, p1, p2, p3, w_ref, o_ref, q_ref, k_ref, v_ref, kept_ref, sent_ref,
                   rows_ref, w_buf, o_buf, mixed_ref, sems):
    copies = load([(w_ref.at[0, i], w_buf.at[i]) for i in range(3)] + [(o_ref.at[0], o_buf)], sems)
    fill((p0, p1, p2, p3), rows_ref)
    for i, out in enumerate((q_ref, k_ref, v_ref)):
        copies[i].wait()
        for cols in tiles_of(out.shape[1]):
            out[:, cols] = dot(rows_ref[...], w_buf[i, :, cols]).astype(jnp.bfloat16)
    for cols in head_slices(q_ref.shape[1]):
        rounded = softmax(q_ref[:, cols], k_ref[:, cols]).astype(jnp.bfloat16)
        mixed_ref[:, cols] = dot(rounded, v_ref[:, cols]).astype(jnp.bfloat16)
    copies[3].wait()
    half = kept_ref.shape[0]
    for cols in tiles_of(o_buf.shape[1]):
        part = dot(mixed_ref[...], o_buf[:, cols])
        kept_ref[:, cols] = part[:half]
        sent_ref[:, cols] = part[half:].astype(jnp.bfloat16)


def backward_kernel(dec_ref, p0, p1, p2, p3, w_ref, q_ref, own_k, own_v, dm_ref,
                    k_ref, mixed_ref, ds_ref, kept_ref, sent_ref,
                    rows_ref, w_buf, v_ref, dk_ref, dv_ref, sems):
    copies = load([(w_ref.at[0, i + 1], w_buf.at[i]) for i in range(2)], sems)
    fill((p0, p1, p2, p3), rows_ref)
    decoder = dec_ref[0] == 1
    for i, (out, own) in enumerate(((k_ref, own_k), (v_ref, own_v))):
        copies[i].wait()
        for cols in tiles_of(out.shape[1]):
            made = dot(rows_ref[...], w_buf[i, :, cols]).astype(jnp.bfloat16)
            out[:, cols] = jnp.where(decoder, made, own[:, cols])
    for cols in head_slices(q_ref.shape[1]):
        q, k, v, dm = q_ref[:, cols], k_ref[:, cols], v_ref[:, cols], dm_ref[:, cols]
        attention = softmax(q, k)
        rounded = attention.astype(jnp.bfloat16)
        mixed_ref[:, cols] = dot(rounded, v).astype(jnp.bfloat16)
        d_rounded = dot_t(dm, v)
        dv_ref[:, cols] = t_dot(rounded, dm).astype(jnp.bfloat16)
        d_scores = attention * (d_rounded - jnp.sum(d_rounded * attention, axis=-1, keepdims=True))
        d_scores = (d_scores * SCALE).astype(jnp.bfloat16)
        ds_ref[:, cols] = d_scores
        dk_ref[:, cols] = t_dot(d_scores, q).astype(jnp.bfloat16)
    half = kept_ref.shape[0]
    for cols in tiles_of(kept_ref.shape[1]):
        part = dot_t(dk_ref[...], w_buf[0, cols, :]) + dot_t(dv_ref[...], w_buf[1, cols, :])
        kept_ref[:, cols] = part[:half]
        sent_ref[:, cols] = part[half:].astype(jnp.bfloat16)


def rest_kernel(dec_ref, k_ref, mixed_ref, ds_ref, w_ref, o_ref, src_kept, src_sent,
                kept_ref, sent_ref, out_kept, out_sent, w_buf, o_buf, dq_ref, sems):
    copies = load([(w_ref.at[0, 0], w_buf), (o_ref.at[0], o_buf)], sems)
    for cols in head_slices(k_ref.shape[1]):
        dq_ref[:, cols] = dot(ds_ref[:, cols], k_ref[:, cols]).astype(jnp.bfloat16)
    encoder = dec_ref[0] == 0
    half = kept_ref.shape[0]
    copies[0].wait()
    for cols in tiles_of(kept_ref.shape[1]):
        part = dot_t(dq_ref[...], w_buf[cols, :])
        own = jnp.where(encoder, src_kept[:, cols], 0.0)
        kept_ref[:, cols] = part[:half] + own
        own = jnp.where(encoder, src_sent[:, cols].astype(jnp.float32), 0.0)
        sent_ref[:, cols] = (part[half:] + own).astype(jnp.bfloat16)
    copies[1].wait()
    for cols in tiles_of(kept_ref.shape[1]):
        part = dot(mixed_ref[...], o_buf[:, cols])
        out_kept[:, cols] = part[:half]
        out_sent[:, cols] = part[half:].astype(jnp.bfloat16)


def call(kernel, name, args, outs, scratch, gflop):
    spec = {"v": pl.BlockSpec(memory_space=pltpu.VMEM), "a": pl.BlockSpec(memory_space=pl.ANY)}
    spec["s"] = pl.BlockSpec(memory_space=pltpu.SMEM)
    return pl.pallas_call(
        kernel,
        name=name,
        out_shape=[jax.ShapeDtypeStruct(shape, dtype) for shape, dtype in outs],
        in_specs=[spec[kind] for kind, _ in args],
        out_specs=[spec["v"]] * len(outs),
        scratch_shapes=scratch,
        compiler_params=pltpu.CompilerParams(vmem_limit_bytes=32 * 2**20),
        cost_estimate=pl.CostEstimate(
            flops=int(gflop * 1.0e9), bytes_accessed=2**20, transcendentals=2**17
        ),
    )(*[value for _, value in args])


def local(hidden, upstream, w_qkv, w_out, norm_gain, final_gain):
    micros = range(hidden.shape[2])
    rows = hidden.shape[1]
    gain = norm_gain[0]
    section_id = lax.axis_index("section")
    x_id = section_id // (NY * NZ)
    y_id = (section_id // NZ) % NY
    z_id = section_id % NZ
    is_decoder = x_id >= NX // 2
    decoder = is_decoder.astype(jnp.int32).reshape(1)

    bf16, f32 = jnp.bfloat16, jnp.float32
    width, inner = hidden.shape[3], w_qkv.shape[3]
    all_rows = 4 * rows
    whole, narrow = (all_rows, width), (all_rows, inner)
    half = (all_rows // 2, width)
    pair = [(half, f32), (half, bf16)]

    inputs = [hidden[0, :, m] for m in micros]
    grads = [upstream[0, :, m] for m in micros]

    def begin_gather(values):
        return [chip_swap(v) for v in values], [core_swap(v) for v in values]

    norms = [normalize(v, gain) for v in inputs]
    others, mates = begin_gather([n[0] for n in norms])
    projections, projected = [], []
    for m in micros:
        *made, kept, sent = call(
            forward_kernel,
            "forward",
            [("v", v) for v in (norms[m][0], others[m], mates[m], core_swap(others[m]))]
            + [("a", w_qkv), ("a", w_out)],
            [(narrow, bf16)] * 3 + pair,
            [
                pltpu.VMEM(whole, bf16),
                pltpu.VMEM(w_qkv.shape[1:], bf16),
                pltpu.VMEM(w_out.shape[1:], bf16),
                pltpu.VMEM(narrow, bf16),
                pltpu.SemaphoreType.DMA((4,)),
            ],
            2.3,
        )
        if m == 0:
            kept, sent, others[1] = together(kept, sent, others[1])
        projections.append(made)
        projected.append((kept, sent))
    enc_out = [
        (v.astype(jnp.float32) + scatter_sum(*p)).astype(jnp.bfloat16)
        for v, p in zip(inputs, projected)
    ]
    enc_out, grads = together(jnp.concatenate(enc_out, axis=1), grads)
    held = spread_pieces(enc_out, x_id, y_id)
    grad_others = [chip_swap(g) for g in grads]
    held, grad_others = together(held, grad_others)
    enc_last = spread_columns(spread_levels(held, z_id), x_id, y_id)

    memories = [
        normalize(enc_last[:, m * width : (m + 1) * width], final_gain)[0] for m in micros
    ]
    others, mates = begin_gather(memories)
    d_mixed = []
    for g, o in zip(grads, grad_others):
        whole_grad = jnp.concatenate([g, o, core_swap(g), core_swap(o)], axis=0)
        d_mixed.append(dot_t(whole_grad, w_out[0]).astype(bf16))
    partials, saved = [], []
    for m in micros:
        query, own_keys, own_values = projections[m]
        keys, mixed, d_scores, kept, sent = call(
            backward_kernel,
            "backward",
            [("s", decoder)]
            + [("v", v) for v in (memories[m], others[m], mates[m], core_swap(others[m]))]
            + [("a", w_qkv)]
            + [("v", v) for v in (query, own_keys, own_values, d_mixed[m])],
            [(narrow, bf16)] * 3 + pair,
            [
                pltpu.VMEM(whole, bf16),
                pltpu.VMEM((2,) + w_qkv.shape[2:], bf16),
                pltpu.VMEM(narrow, bf16),
                pltpu.VMEM(narrow, bf16),
                pltpu.VMEM(narrow, bf16),
                pltpu.SemaphoreType.DMA((2,)),
            ],
            2.5,
        )
        rest = (keys, mixed, d_scores)
        if m == 0:
            kept, sent, others[1] = together(kept, sent, others[1])
        else:
            kept, sent, rest, saved[0] = together(kept, sent, rest, saved[0])
        partials.append((kept, sent))
        saved.append(rest)
    first = sum_cores(*partials[0])
    first, saved = together(first, saved)

    rests = []
    for m in micros:
        made = call(
            rest_kernel,
            "rest",
            [("s", decoder)]
            + [("v", v) for v in saved[m]]
            + [("a", w_qkv), ("a", w_out)]
            + [("v", v) for v in partials[m]],
            pair * 2,
            [
                pltpu.VMEM(w_qkv.shape[2:], bf16),
                pltpu.VMEM(w_out.shape[1:], bf16),
                pltpu.VMEM(narrow, bf16),
                pltpu.SemaphoreType.DMA((2,)),
            ],
            1.2,
        )
        rests += [sum_cores(*made[:2]), sum_cores(*made[2:])]
    total = [sum_chips(*first), scatter_sum(*partials[1])]
    total = jnp.concatenate(total, axis=1)
    quarter, eighth = rows // NX, rows // (NX * NY)

    def quarter_of(v, x):
        return lax.dynamic_slice_in_dim(v, x * quarter, quarter, axis=0)

    def eighth_of(v, y):
        return lax.dynamic_slice_in_dim(v, y * eighth, eighth, axis=0)

    got = move(quarter_of(enc_last, x_id ^ 3), x_perm(3, (2, 3)))
    last = eighth_of(jnp.where(is_decoder, quarter_of(enc_last, x_id), got), y_id)
    total = jnp.where(is_decoder, total, 0.0)
    wire = total.astype(bf16)
    total, last, rests = together(total, last, rests)
    rests = [sum_chips(*v) for v in rests]

    last = [last[:, : last.shape[1] // 2], last[:, last.shape[1] // 2 :]]
    total = quarter_of(total, x_id)
    for k in (1, 2, 3):
        got = move(quarter_of(wire, x_id ^ k), x_perm(k, (2, 3)))
        total = total + got.astype(jnp.float32)
    got = jump(eighth_of(total, y_id ^ 1).astype(jnp.bfloat16), Y_NEXT)
    total = eighth_of(total, y_id) + got.astype(jnp.float32)
    for k in (4, 2, 1):
        if k == 1:
            total, rests[0] = together(total, rests[0])
        wire = total.astype(jnp.bfloat16)
        total = wire.astype(jnp.float32) + move(wire, z_swap(k)).astype(jnp.float32)
    total, rests[1] = together(total, rests[1])
    total = [total[:, : total.shape[1] // 2], total[:, total.shape[1] // 2 :]]
    out = []
    for m in micros:
        inverse = normalize(last[m], final_gain)[1]
        out.append(norm_back(last[m], inverse, total[m] * final_gain, 0.0).astype(jnp.bfloat16))
    out = jnp.concatenate(out, axis=1)
    got, first = jump(out, Y_BACK), jump(out, Y_PAIR)
    out = jnp.where(
        y_id == 0, jnp.concatenate([first, got], axis=0), jnp.concatenate([got, out], axis=0)
    )
    out, rests[2] = together(out, rests[2])
    section_out, grad_in = [], []
    for m in micros:
        d_normed, summed = rests[2 * m], rests[2 * m + 1]
        base = grads[m].astype(jnp.float32)
        base = norm_back(inputs[m], norms[m][1], d_normed * gain, base)
        grad_in.append(base.astype(jnp.bfloat16))
        section_out.append((inputs[m].astype(jnp.float32) + summed).astype(jnp.bfloat16))
    parts = [out] + [move(out, x_perm(k, range(NX))) for k in (1, 2, 3)]
    odd, high = (x_id & 1) == 1, (x_id & 2) == 2
    parts = [jnp.where(odd, parts[j ^ 1], parts[j]) for j in range(NX)]
    parts = [jnp.where(high, parts[j ^ 2], parts[j]) for j in range(NX)]
    out = jnp.concatenate(parts, axis=0)
    memory_grad_out = [out[:, : out.shape[1] // 2], out[:, out.shape[1] // 2 :]]

    return tuple(
        jnp.stack(v, axis=1)[None] for v in (section_out, grad_in, memory_grad_out)
    )


def solution(mesh):
    in_specs = (
        P("section", "tp", None, None),
        P("section", "tp", None, None),
        P("section", None, None, "tp"),
        P("section", "tp", None),
        P("section", None),
        P(),
    )
    out_specs = (
        P("section", "tp", None, None),
        P("section", "tp", None, None),
        P("section", "tp", None, None),
    )
    return jax.shard_map(local, mesh=mesh, in_specs=in_specs, out_specs=out_specs, check_vma=False)
```

```python
import jax
import jax.numpy as jnp
from jax import lax
from jax.experimental import pallas as pl
from jax.experimental.pallas import tpu as pltpu
from jax.sharding import PartitionSpec as P

HEAD_DIM = 256
epsilon = 1e-06

NX, NY, NZ = 4, 2, 8
CORE_SWAP = [(t, t ^ 1) for t in range(4)]
CHIP_SWAP = [(t, t ^ 2) for t in range(4)]


def sec(x, y, z):
    return (x * NY + y) * NZ + z


def x_perm(k, sources):
    return [(sec(x, y, z), sec(x ^ k, y, z)) for x in sources for y in range(NY) for z in range(NZ)]


def across(pairs):
    def index(x, y, z, low, core):
        return 4 * sec(x, y, z) + 2 * low + core

    return [
        (index(x, a[0], z, a[1], core), index(x, b[0], z, b[1], core))
        for a, b in pairs
        for x in range(NX)
        for z in range(NZ)
        for core in range(2)
    ]


Y_NEXT = across([((y, low), (1 - y, 1 - low)) for y in range(2) for low in range(2)])
Y_BACK = across(
    [((1, low), (0, low)) for low in range(2)] + [((0, low), (1, 1 - low)) for low in range(2)]
)
Y_PAIR = across([((0, low), (0, 1 - low)) for low in range(2)])


def jump(rows, pairs):
    return lax.ppermute(rows, ("section", "tp"), pairs)


def z_swap(k):
    return [(sec(x, y, z), sec(x, y, z ^ k)) for x in range(NX) for y in range(NY) for z in range(NZ)]


def dot(a, b):
    return jnp.dot(a, b, preferred_element_type=jnp.float32)


def dot_t(a, b):
    return lax.dot_general(a, b, (((1,), (1,)), ((), ())), preferred_element_type=jnp.float32)


def t_dot(a, b):
    return lax.dot_general(a, b, (((0,), (0,)), ((), ())), preferred_element_type=jnp.float32)


def normalize(inputs, gain):
    values = inputs.astype(jnp.float32)
    inverse = lax.rsqrt(jnp.mean(values * values, axis=-1, keepdims=True) + epsilon)
    return ((values * inverse * gain).astype(jnp.bfloat16), inverse)


def norm_back(inputs, inverse, d_normed, base):
    values = inputs.astype(jnp.float32)
    inner_mean = jnp.mean(values * d_normed, axis=-1, keepdims=True)
    return base + inverse * d_normed - values * inverse * inverse * inverse * inner_mean


def chip_swap(rows):
    return lax.ppermute(rows, "tp", CHIP_SWAP)


def core_swap(rows):
    return lax.ppermute(rows, "tp", CORE_SWAP)


def gather_rows(rows):
    other = chip_swap(rows)
    return jnp.concatenate([rows, other, core_swap(rows), core_swap(other)], axis=0)


def halves(rows):
    count = rows.shape[0] // 2
    return rows[:count], rows[count:]


def sum_cores(kept, sent):
    kept, sent = halves(kept + core_swap(sent.astype(jnp.bfloat16)).astype(jnp.float32))
    return kept, sent.astype(jnp.bfloat16)


def sum_chips(kept, sent):
    return kept + chip_swap(sent).astype(jnp.float32)


def scatter_sum(kept, sent):
    return sum_chips(*sum_cores(kept, sent))


def together(*values):
    return lax.optimization_barrier(values)


def move(rows, pairs):
    return lax.ppermute(rows, "section", pairs)


def ordered(mine, got, first):
    return jnp.where(
        first, jnp.concatenate([mine, got], axis=0), jnp.concatenate([got, mine], axis=0)
    )


def spread_pieces(rows, x_id, y_id):
    count = rows.shape[0] // 4
    held = None
    for index in (2, 0, 3, 1):
        x, y = 2 + index // 2, index % 2
        piece = rows[index * count : (index + 1) * count]
        root, target = 4 * sec(1, 1, 7), 4 * sec(x, y, 7)
        got = jump(piece, [(root + t, target + (t if y else t ^ 2)) for t in range(4)])
        held = got if held is None else jnp.where((x_id == x) & (y_id == y), got, held)
    return held


def z_pairs(*hops):
    return [(sec(x, y, a), sec(x, y, b)) for x in (2, 3) for y in range(NY) for a, b in hops]


def spread_levels(held, z_id):
    five = move(held, z_pairs((7, 5)))
    one = move(held, z_pairs((7, 1)))
    return jnp.where(z_id == 5, five, jnp.where(z_id == 1, one, held))


def spread_near(held, z_id):
    far = move(held, z_pairs((1, 3), (5, 4)))
    near = move(held, z_pairs((7, 0), (1, 2), (5, 6)))
    from_far = (z_id == 3) | (z_id == 4)
    from_near = (z_id == 0) | (z_id == 2) | (z_id == 6)
    held = jnp.where(from_far, far, jnp.where(from_near, near, held))
    return held


def spread_columns(held, x_id, y_id):
    held = ordered(held, jump(held, Y_NEXT), y_id == 0)
    return ordered(held, move(held, x_perm(1, (2, 3))), x_id == 2)


SCALE = HEAD_DIM ** (-0.5)
TILE = 512


def head_slices(width):
    return [slice(h * HEAD_DIM, (h + 1) * HEAD_DIM) for h in range(width // HEAD_DIM)]


def softmax(q, k):
    scores = dot_t(q, k) * SCALE
    raised = jnp.exp(scores - jnp.max(scores, axis=-1, keepdims=True))
    return raised / jnp.sum(raised, axis=-1, keepdims=True)


def fill(pieces, rows_ref):
    count = rows_ref.shape[0] // len(pieces)
    for i, piece in enumerate(pieces):
        rows_ref[i * count : (i + 1) * count, :] = piece[...]


def load(pairs, sems):
    copies = [pltpu.make_async_copy(a, b, sems.at[i]) for i, (a, b) in enumerate(pairs)]
    for copy in copies:
        copy.start()
    return copies


def tiles_of(width):
    return [slice(t, t + TILE) for t in range(0, width, TILE)]


def forward_kernel(p0, p1, p2, p3, w_ref, o_ref, q_ref, k_ref, v_ref, kept_ref, sent_ref,
                   rows_ref, w_buf, o_buf, mixed_ref, sems):
    copies = load([(w_ref.at[0, i], w_buf.at[i]) for i in range(3)] + [(o_ref.at[0], o_buf)], sems)
    fill((p0, p1, p2, p3), rows_ref)
    for i, out in enumerate((q_ref, k_ref, v_ref)):
        copies[i].wait()
        for cols in tiles_of(out.shape[1]):
            out[:, cols] = dot(rows_ref[...], w_buf[i, :, cols]).astype(jnp.bfloat16)
    for cols in head_slices(q_ref.shape[1]):
        rounded = softmax(q_ref[:, cols], k_ref[:, cols]).astype(jnp.bfloat16)
        mixed_ref[:, cols] = dot(rounded, v_ref[:, cols]).astype(jnp.bfloat16)
    copies[3].wait()
    half = kept_ref.shape[0]
    for cols in tiles_of(o_buf.shape[1]):
        part = dot(mixed_ref[...], o_buf[:, cols])
        kept_ref[:, cols] = part[:half]
        sent_ref[:, cols] = part[half:].astype(jnp.bfloat16)


def backward_kernel(dec_ref, p0, p1, p2, p3, w_ref, q_ref, own_k, own_v, dm_ref,
                    k_ref, mixed_ref, ds_ref, kept_ref, sent_ref,
                    rows_ref, w_buf, v_ref, dk_ref, dv_ref, sems):
    copies = load([(w_ref.at[0, i + 1], w_buf.at[i]) for i in range(2)], sems)
    fill((p0, p1, p2, p3), rows_ref)
    decoder = dec_ref[0] == 1
    for i, (out, own) in enumerate(((k_ref, own_k), (v_ref, own_v))):
        copies[i].wait()
        for cols in tiles_of(out.shape[1]):
            made = dot(rows_ref[...], w_buf[i, :, cols]).astype(jnp.bfloat16)
            out[:, cols] = jnp.where(decoder, made, own[:, cols])
    for cols in head_slices(q_ref.shape[1]):
        q, k, v, dm = q_ref[:, cols], k_ref[:, cols], v_ref[:, cols], dm_ref[:, cols]
        attention = softmax(q, k)
        rounded = attention.astype(jnp.bfloat16)
        mixed_ref[:, cols] = dot(rounded, v).astype(jnp.bfloat16)
        d_rounded = dot_t(dm, v)
        dv_ref[:, cols] = t_dot(rounded, dm).astype(jnp.bfloat16)
        d_scores = attention * (d_rounded - jnp.sum(d_rounded * attention, axis=-1, keepdims=True))
        d_scores = (d_scores * SCALE).astype(jnp.bfloat16)
        ds_ref[:, cols] = d_scores
        dk_ref[:, cols] = t_dot(d_scores, q).astype(jnp.bfloat16)
    half = kept_ref.shape[0]
    for cols in tiles_of(kept_ref.shape[1]):
        part = dot_t(dk_ref[...], w_buf[0, cols, :]) + dot_t(dv_ref[...], w_buf[1, cols, :])
        kept_ref[:, cols] = part[:half]
        sent_ref[:, cols] = part[half:].astype(jnp.bfloat16)


def rest_kernel(dec_ref, k_ref, mixed_ref, ds_ref, w_ref, o_ref, src_kept, src_sent,
                kept_ref, sent_ref, out_kept, out_sent, w_buf, o_buf, dq_ref, sems):
    copies = load([(w_ref.at[0, 0], w_buf), (o_ref.at[0], o_buf)], sems)
    for cols in head_slices(k_ref.shape[1]):
        dq_ref[:, cols] = dot(ds_ref[:, cols], k_ref[:, cols]).astype(jnp.bfloat16)
    encoder = dec_ref[0] == 0
    half = kept_ref.shape[0]
    copies[0].wait()
    for cols in tiles_of(kept_ref.shape[1]):
        part = dot_t(dq_ref[...], w_buf[cols, :])
        own = jnp.where(encoder, src_kept[:, cols], 0.0)
        kept_ref[:, cols] = part[:half] + own
        own = jnp.where(encoder, src_sent[:, cols].astype(jnp.float32), 0.0)
        sent_ref[:, cols] = (part[half:] + own).astype(jnp.bfloat16)
    copies[1].wait()
    for cols in tiles_of(kept_ref.shape[1]):
        part = dot(mixed_ref[...], o_buf[:, cols])
        out_kept[:, cols] = part[:half]
        out_sent[:, cols] = part[half:].astype(jnp.bfloat16)


def call(kernel, name, args, outs, scratch, gflop):
    spec = {"v": pl.BlockSpec(memory_space=pltpu.VMEM), "a": pl.BlockSpec(memory_space=pl.ANY)}
    spec["s"] = pl.BlockSpec(memory_space=pltpu.SMEM)
    return pl.pallas_call(
        kernel,
        name=name,
        out_shape=[jax.ShapeDtypeStruct(shape, dtype) for shape, dtype in outs],
        in_specs=[spec[kind] for kind, _ in args],
        out_specs=[spec["v"]] * len(outs),
        scratch_shapes=scratch,
        compiler_params=pltpu.CompilerParams(vmem_limit_bytes=32 * 2**20),
        cost_estimate=pl.CostEstimate(
            flops=int(gflop * 1.0e9), bytes_accessed=2**20, transcendentals=2**17
        ),
    )(*[value for _, value in args])


def local(hidden, upstream, w_qkv, w_out, norm_gain, final_gain):
    micros = range(hidden.shape[2])
    rows = hidden.shape[1]
    gain = norm_gain[0]
    section_id = lax.axis_index("section")
    x_id = section_id // (NY * NZ)
    y_id = (section_id // NZ) % NY
    z_id = section_id % NZ
    is_decoder = x_id >= NX // 2
    decoder = is_decoder.astype(jnp.int32).reshape(1)

    bf16, f32 = jnp.bfloat16, jnp.float32
    width, inner = hidden.shape[3], w_qkv.shape[3]
    all_rows = 4 * rows
    whole, narrow = (all_rows, width), (all_rows, inner)
    half = (all_rows // 2, width)
    pair = [(half, f32), (half, bf16)]

    inputs = [hidden[0, :, m] for m in micros]
    grads = [upstream[0, :, m] for m in micros]

    def begin_gather(values):
        return [chip_swap(v) for v in values], [core_swap(v) for v in values]

    norms = [normalize(v, gain) for v in inputs]
    others, mates = begin_gather([n[0] for n in norms])
    projections, projected = [], []
    for m in micros:
        *made, kept, sent = call(
            forward_kernel,
            "forward",
            [("v", v) for v in (norms[m][0], others[m], mates[m], core_swap(others[m]))]
            + [("a", w_qkv), ("a", w_out)],
            [(narrow, bf16)] * 3 + pair,
            [
                pltpu.VMEM(whole, bf16),
                pltpu.VMEM(w_qkv.shape[1:], bf16),
                pltpu.VMEM(w_out.shape[1:], bf16),
                pltpu.VMEM(narrow, bf16),
                pltpu.SemaphoreType.DMA((4,)),
            ],
            2.3,
        )
        if m == 0:
            kept, sent, others[1] = together(kept, sent, others[1])
        projections.append(made)
        projected.append((kept, sent))
    enc_out = [
        (v.astype(jnp.float32) + scatter_sum(*p)).astype(jnp.bfloat16)
        for v, p in zip(inputs, projected)
    ]
    enc_out, grads = together(jnp.concatenate(enc_out, axis=1), grads)
    held = spread_pieces(enc_out, x_id, y_id)
    grad_others = [chip_swap(grads[0])]
    held, grad_others[0], grads[1] = together(held, grad_others[0], grads[1])
    held = spread_levels(held, z_id)
    grad_others.append(chip_swap(grads[1]))
    held, grad_others[1] = together(held, grad_others[1])
    enc_last = spread_columns(spread_near(held, z_id), x_id, y_id)

    memories = [
        normalize(enc_last[:, m * width : (m + 1) * width], final_gain)[0] for m in micros
    ]
    others, mates = begin_gather(memories)
    d_mixed = []
    for g, o in zip(grads, grad_others):
        whole_grad = jnp.concatenate([g, o, core_swap(g), core_swap(o)], axis=0)
        d_mixed.append(dot_t(whole_grad, w_out[0]).astype(bf16))
    partials, saved = [], []
    for m in micros:
        query, own_keys, own_values = projections[m]
        keys, mixed, d_scores, kept, sent = call(
            backward_kernel,
            "backward",
            [("s", decoder)]
            + [("v", v) for v in (memories[m], others[m], mates[m], core_swap(others[m]))]
            + [("a", w_qkv)]
            + [("v", v) for v in (query, own_keys, own_values, d_mixed[m])],
            [(narrow, bf16)] * 3 + pair,
            [
                pltpu.VMEM(whole, bf16),
                pltpu.VMEM((2,) + w_qkv.shape[2:], bf16),
                pltpu.VMEM(narrow, bf16),
                pltpu.VMEM(narrow, bf16),
                pltpu.VMEM(narrow, bf16),
                pltpu.SemaphoreType.DMA((2,)),
            ],
            2.5,
        )
        rest = (keys, mixed, d_scores)
        if m == 0:
            kept, sent, others[1] = together(kept, sent, others[1])
        else:
            kept, sent, rest, saved[0] = together(kept, sent, rest, saved[0])
        partials.append((kept, sent))
        saved.append(rest)
    first = sum_cores(*partials[0])
    first, saved = together(first, saved)

    rests = []
    for m in micros:
        made = call(
            rest_kernel,
            "rest",
            [("s", decoder)]
            + [("v", v) for v in saved[m]]
            + [("a", w_qkv), ("a", w_out)]
            + [("v", v) for v in partials[m]],
            pair * 2,
            [
                pltpu.VMEM(w_qkv.shape[2:], bf16),
                pltpu.VMEM(w_out.shape[1:], bf16),
                pltpu.VMEM(narrow, bf16),
                pltpu.SemaphoreType.DMA((2,)),
            ],
            1.2,
        )
        rests += [sum_cores(*made[:2]), sum_cores(*made[2:])]
    total = [sum_chips(*first), scatter_sum(*partials[1])]
    total = jnp.concatenate(total, axis=1)
    quarter, eighth = rows // NX, rows // (NX * NY)

    def quarter_of(v, x):
        return lax.dynamic_slice_in_dim(v, x * quarter, quarter, axis=0)

    def eighth_of(v, y):
        return lax.dynamic_slice_in_dim(v, y * eighth, eighth, axis=0)

    got = move(quarter_of(enc_last, x_id ^ 3), x_perm(3, (2, 3)))
    last = eighth_of(jnp.where(is_decoder, quarter_of(enc_last, x_id), got), y_id)
    total = jnp.where(is_decoder, total, 0.0)
    wire = total.astype(bf16)
    total, last, rests = together(total, last, rests)
    rests = [sum_chips(*v) for v in rests]

    last = [last[:, : last.shape[1] // 2], last[:, last.shape[1] // 2 :]]
    total = quarter_of(total, x_id)
    for k in (1, 2, 3):
        got = move(quarter_of(wire, x_id ^ k), x_perm(k, (2, 3)))
        total = total + got.astype(jnp.float32)
    got = jump(eighth_of(total, y_id ^ 1).astype(jnp.bfloat16), Y_NEXT)
    total = eighth_of(total, y_id) + got.astype(jnp.float32)
    for k in (4, 2, 1):
        if k == 1:
            total, rests[0] = together(total, rests[0])
        wire = total.astype(jnp.bfloat16)
        total = wire.astype(jnp.float32) + move(wire, z_swap(k)).astype(jnp.float32)
    total, rests[1] = together(total, rests[1])
    total = [total[:, : total.shape[1] // 2], total[:, total.shape[1] // 2 :]]
    out = []
    for m in micros:
        inverse = normalize(last[m], final_gain)[1]
        out.append(norm_back(last[m], inverse, total[m] * final_gain, 0.0).astype(jnp.bfloat16))
    out = jnp.concatenate(out, axis=1)
    got, first = jump(out, Y_BACK), jump(out, Y_PAIR)
    out = jnp.where(
        y_id == 0, jnp.concatenate([first, got], axis=0), jnp.concatenate([got, out], axis=0)
    )
    out, rests[2] = together(out, rests[2])
    section_out, grad_in = [], []
    for m in micros:
        d_normed, summed = rests[2 * m], rests[2 * m + 1]
        base = grads[m].astype(jnp.float32)
        base = norm_back(inputs[m], norms[m][1], d_normed * gain, base)
        grad_in.append(base.astype(jnp.bfloat16))
        section_out.append((inputs[m].astype(jnp.float32) + summed).astype(jnp.bfloat16))
    parts = [out] + [move(out, x_perm(k, range(NX))) for k in (1, 2, 3)]
    odd, high = (x_id & 1) == 1, (x_id & 2) == 2
    parts = [jnp.where(odd, parts[j ^ 1], parts[j]) for j in range(NX)]
    parts = [jnp.where(high, parts[j ^ 2], parts[j]) for j in range(NX)]
    out = jnp.concatenate(parts, axis=0)
    memory_grad_out = [out[:, : out.shape[1] // 2], out[:, out.shape[1] // 2 :]]

    return tuple(
        jnp.stack(v, axis=1)[None] for v in (section_out, grad_in, memory_grad_out)
    )


def solution(mesh):
    in_specs = (
        P("section", "tp", None, None),
        P("section", "tp", None, None),
        P("section", None, None, "tp"),
        P("section", "tp", None),
        P("section", None),
        P(),
    )
    out_specs = (
        P("section", "tp", None, None),
        P("section", "tp", None, None),
        P("section", "tp", None, None),
    )
    return jax.shard_map(local, mesh=mesh, in_specs=in_specs, out_specs=out_specs, check_vma=False)
```

```python
import jax
import jax.numpy as jnp
from jax import lax
from jax.experimental import pallas as pl
from jax.experimental.pallas import tpu as pltpu
from jax.sharding import PartitionSpec as P

HEAD_DIM = 256
epsilon = 1e-06

NX, NY, NZ = 4, 2, 8
CORE_SWAP = [(t, t ^ 1) for t in range(4)]
CHIP_SWAP = [(t, t ^ 2) for t in range(4)]


def sec(x, y, z):
    return (x * NY + y) * NZ + z


def x_perm(k, sources):
    return [(sec(x, y, z), sec(x ^ k, y, z)) for x in sources for y in range(NY) for z in range(NZ)]


def across(pairs):
    def index(x, y, z, low, core):
        return 4 * sec(x, y, z) + 2 * low + core

    return [
        (index(x, a[0], z, a[1], core), index(x, b[0], z, b[1], core))
        for a, b in pairs
        for x in range(NX)
        for z in range(NZ)
        for core in range(2)
    ]


Y_NEXT = across([((y, low), (1 - y, 1 - low)) for y in range(2) for low in range(2)])
Y_BACK = across(
    [((1, low), (0, low)) for low in range(2)] + [((0, low), (1, 1 - low)) for low in range(2)]
)
Y_PAIR = across([((0, low), (0, 1 - low)) for low in range(2)])


def jump(rows, pairs):
    return lax.ppermute(rows, ("section", "tp"), pairs)


def z_swap(k):
    return [(sec(x, y, z), sec(x, y, z ^ k)) for x in range(NX) for y in range(NY) for z in range(NZ)]


def dot(a, b):
    return jnp.dot(a, b, preferred_element_type=jnp.float32)


def dot_t(a, b):
    return lax.dot_general(a, b, (((1,), (1,)), ((), ())), preferred_element_type=jnp.float32)


def t_dot(a, b):
    return lax.dot_general(a, b, (((0,), (0,)), ((), ())), preferred_element_type=jnp.float32)


def normalize(inputs, gain):
    values = inputs.astype(jnp.float32)
    inverse = lax.rsqrt(jnp.mean(values * values, axis=-1, keepdims=True) + epsilon)
    return ((values * inverse * gain).astype(jnp.bfloat16), inverse)


def norm_back(inputs, inverse, d_normed, base):
    values = inputs.astype(jnp.float32)
    inner_mean = jnp.mean(values * d_normed, axis=-1, keepdims=True)
    return base + inverse * d_normed - values * inverse * inverse * inverse * inner_mean


def chip_swap(rows):
    return lax.ppermute(rows, "tp", CHIP_SWAP)


def core_swap(rows):
    return lax.ppermute(rows, "tp", CORE_SWAP)


def gather_rows(rows):
    other = chip_swap(rows)
    return jnp.concatenate([rows, other, core_swap(rows), core_swap(other)], axis=0)


def halves(rows):
    count = rows.shape[0] // 2
    return rows[:count], rows[count:]


def sum_cores(kept, sent):
    kept, sent = halves(kept + core_swap(sent.astype(jnp.bfloat16)).astype(jnp.float32))
    return kept, sent.astype(jnp.bfloat16)


def sum_chips(kept, sent):
    return kept + chip_swap(sent).astype(jnp.float32)


def scatter_sum(kept, sent):
    return sum_chips(*sum_cores(kept, sent))


def together(*values):
    return lax.optimization_barrier(values)


def move(rows, pairs):
    return lax.ppermute(rows, "section", pairs)


def ordered(mine, got, first):
    return jnp.where(
        first, jnp.concatenate([mine, got], axis=0), jnp.concatenate([got, mine], axis=0)
    )


def spread_pieces(rows, x_id, y_id):
    count = rows.shape[0] // 4
    held = None
    for index in (2, 0, 3, 1):
        x, y = 2 + index // 2, index % 2
        piece = rows[index * count : (index + 1) * count]
        root, target = 4 * sec(1, 1, 7), 4 * sec(x, y, 7)
        got = jump(piece, [(root + t, target + (t if y else t ^ 2)) for t in range(4)])
        held = got if held is None else jnp.where((x_id == x) & (y_id == y), got, held)
    return held


def z_pairs(*hops):
    return [(sec(x, y, a), sec(x, y, b)) for x in (2, 3) for y in range(NY) for a, b in hops]


def spread_levels(held, z_id):
    five = move(held, z_pairs((7, 5)))
    one = move(held, z_pairs((7, 1)))
    return jnp.where(z_id == 5, five, jnp.where(z_id == 1, one, held))


def spread_near(held, z_id):
    far = move(held, z_pairs((1, 3), (5, 4)))
    near = move(held, z_pairs((7, 0), (1, 2), (5, 6)))
    from_far = (z_id == 3) | (z_id == 4)
    from_near = (z_id == 0) | (z_id == 2) | (z_id == 6)
    held = jnp.where(from_far, far, jnp.where(from_near, near, held))
    return held


def spread_columns(held, x_id, y_id):
    held = ordered(held, jump(held, Y_NEXT), y_id == 0)
    return ordered(held, move(held, x_perm(1, (2, 3))), x_id == 2)


SCALE = HEAD_DIM ** (-0.5)
TILE = 512


def head_slices(width):
    return [slice(h * HEAD_DIM, (h + 1) * HEAD_DIM) for h in range(width // HEAD_DIM)]


def softmax(q, k):
    scores = dot_t(q, k) * SCALE
    raised = jnp.exp(scores - jnp.max(scores, axis=-1, keepdims=True))
    return raised / jnp.sum(raised, axis=-1, keepdims=True)


def fill(pieces, rows_ref):
    count = rows_ref.shape[0] // len(pieces)
    for i, piece in enumerate(pieces):
        rows_ref[i * count : (i + 1) * count, :] = piece[...]


def load(pairs, sems):
    copies = [pltpu.make_async_copy(a, b, sems.at[i]) for i, (a, b) in enumerate(pairs)]
    for copy in copies:
        copy.start()
    return copies


def tiles_of(width):
    return [slice(t, t + TILE) for t in range(0, width, TILE)]


def forward_kernel(p0, p1, p2, p3, w_ref, o_ref, q_ref, k_ref, v_ref, kept_ref, sent_ref,
                   rows_ref, mixed_ref):
    fill((p0, p1, p2, p3), rows_ref)
    for i, out in enumerate((q_ref, k_ref, v_ref)):
        for cols in tiles_of(out.shape[1]):
            out[:, cols] = dot(rows_ref[...], w_ref[0, i, :, cols]).astype(jnp.bfloat16)
    for cols in head_slices(q_ref.shape[1]):
        rounded = softmax(q_ref[:, cols], k_ref[:, cols]).astype(jnp.bfloat16)
        mixed_ref[:, cols] = dot(rounded, v_ref[:, cols]).astype(jnp.bfloat16)
    half = kept_ref.shape[0]
    for cols in tiles_of(o_ref.shape[2]):
        part = dot(mixed_ref[...], o_ref[0, :, cols])
        kept_ref[:, cols] = part[:half]
        sent_ref[:, cols] = part[half:].astype(jnp.bfloat16)


def backward_kernel(dec_ref, p0, p1, p2, p3, w_ref, q_ref, own_k, own_v, dm_ref,
                    k_ref, mixed_ref, ds_ref, kept_ref, sent_ref,
                    rows_ref, w_buf, v_ref, dk_ref, dv_ref, sems):
    copies = load([(w_ref.at[0, i + 1], w_buf.at[i]) for i in range(2)], sems)
    fill((p0, p1, p2, p3), rows_ref)
    decoder = dec_ref[0] == 1
    for i, (out, own) in enumerate(((k_ref, own_k), (v_ref, own_v))):
        copies[i].wait()
        for cols in tiles_of(out.shape[1]):
            made = dot(rows_ref[...], w_buf[i, :, cols]).astype(jnp.bfloat16)
            out[:, cols] = jnp.where(decoder, made, own[:, cols])
    for cols in head_slices(q_ref.shape[1]):
        q, k, v, dm = q_ref[:, cols], k_ref[:, cols], v_ref[:, cols], dm_ref[:, cols]
        attention = softmax(q, k)
        rounded = attention.astype(jnp.bfloat16)
        mixed_ref[:, cols] = dot(rounded, v).astype(jnp.bfloat16)
        d_rounded = dot_t(dm, v)
        dv_ref[:, cols] = t_dot(rounded, dm).astype(jnp.bfloat16)
        d_scores = attention * (d_rounded - jnp.sum(d_rounded * attention, axis=-1, keepdims=True))
        d_scores = (d_scores * SCALE).astype(jnp.bfloat16)
        ds_ref[:, cols] = d_scores
        dk_ref[:, cols] = t_dot(d_scores, q).astype(jnp.bfloat16)
    half = kept_ref.shape[0]
    for cols in tiles_of(kept_ref.shape[1]):
        part = dot_t(dk_ref[...], w_buf[0, cols, :]) + dot_t(dv_ref[...], w_buf[1, cols, :])
        kept_ref[:, cols] = part[:half]
        sent_ref[:, cols] = part[half:].astype(jnp.bfloat16)


def rest_kernel(dec_ref, k_ref, mixed_ref, ds_ref, w_ref, o_ref, src_kept, src_sent,
                kept_ref, sent_ref, out_kept, out_sent, w_buf, o_buf, dq_ref, sems):
    copies = load([(w_ref.at[0, 0], w_buf), (o_ref.at[0], o_buf)], sems)
    for cols in head_slices(k_ref.shape[1]):
        dq_ref[:, cols] = dot(ds_ref[:, cols], k_ref[:, cols]).astype(jnp.bfloat16)
    encoder = dec_ref[0] == 0
    half = kept_ref.shape[0]
    copies[0].wait()
    for cols in tiles_of(kept_ref.shape[1]):
        part = dot_t(dq_ref[...], w_buf[cols, :])
        own = jnp.where(encoder, src_kept[:, cols], 0.0)
        kept_ref[:, cols] = part[:half] + own
        own = jnp.where(encoder, src_sent[:, cols].astype(jnp.float32), 0.0)
        sent_ref[:, cols] = (part[half:] + own).astype(jnp.bfloat16)
    copies[1].wait()
    for cols in tiles_of(kept_ref.shape[1]):
        part = dot(mixed_ref[...], o_buf[:, cols])
        out_kept[:, cols] = part[:half]
        out_sent[:, cols] = part[half:].astype(jnp.bfloat16)


def call(kernel, name, args, outs, scratch, gflop):
    spec = {"v": pl.BlockSpec(memory_space=pltpu.VMEM), "a": pl.BlockSpec(memory_space=pl.ANY)}
    spec["s"] = pl.BlockSpec(memory_space=pltpu.SMEM)
    return pl.pallas_call(
        kernel,
        name=name,
        out_shape=[jax.ShapeDtypeStruct(shape, dtype) for shape, dtype in outs],
        in_specs=[spec[kind] for kind, _ in args],
        out_specs=[spec["v"]] * len(outs),
        scratch_shapes=scratch,
        compiler_params=pltpu.CompilerParams(vmem_limit_bytes=32 * 2**20),
        cost_estimate=pl.CostEstimate(
            flops=int(gflop * 1.0e9), bytes_accessed=2**20, transcendentals=2**17
        ),
    )(*[value for _, value in args])


def local(hidden, upstream, w_qkv, w_out, norm_gain, final_gain):
    micros = range(hidden.shape[2])
    rows = hidden.shape[1]
    gain = norm_gain[0]
    section_id = lax.axis_index("section")
    x_id = section_id // (NY * NZ)
    y_id = (section_id // NZ) % NY
    z_id = section_id % NZ
    is_decoder = x_id >= NX // 2
    decoder = is_decoder.astype(jnp.int32).reshape(1)

    bf16, f32 = jnp.bfloat16, jnp.float32
    width, inner = hidden.shape[3], w_qkv.shape[3]
    all_rows = 4 * rows
    whole, narrow = (all_rows, width), (all_rows, inner)
    half = (all_rows // 2, width)
    pair = [(half, f32), (half, bf16)]

    inputs = [hidden[0, :, m] for m in micros]
    grads = [upstream[0, :, m] for m in micros]

    def begin_gather(values):
        return [chip_swap(v) for v in values], [core_swap(v) for v in values]

    norms = [normalize(v, gain) for v in inputs]
    others, mates = begin_gather([n[0] for n in norms])
    projections, projected = [], []
    for m in micros:
        *made, kept, sent = call(
            forward_kernel,
            "forward",
            [("v", v) for v in (norms[m][0], others[m], mates[m], core_swap(others[m]))]
            + [("v", w_qkv), ("v", w_out)],
            [(narrow, bf16)] * 3 + pair,
            [pltpu.VMEM(whole, bf16), pltpu.VMEM(narrow, bf16)],
            2.3,
        )
        if m == 0:
            kept, sent, others[1] = together(kept, sent, others[1])
        projections.append(made)
        projected.append((kept, sent))
    enc_out = [
        (v.astype(jnp.float32) + scatter_sum(*p)).astype(jnp.bfloat16)
        for v, p in zip(inputs, projected)
    ]
    enc_out, grads = together(jnp.concatenate(enc_out, axis=1), grads)
    held = spread_pieces(enc_out, x_id, y_id)
    grad_others = [chip_swap(grads[0])]
    held, grad_others[0], grads[1] = together(held, grad_others[0], grads[1])
    held = spread_levels(held, z_id)
    grad_others.append(chip_swap(grads[1]))
    held, grad_others[1] = together(held, grad_others[1])
    enc_last = spread_columns(spread_near(held, z_id), x_id, y_id)

    memories = [
        normalize(enc_last[:, m * width : (m + 1) * width], final_gain)[0] for m in micros
    ]
    others, mates = begin_gather(memories)
    d_mixed = []
    for g, o in zip(grads, grad_others):
        whole_grad = jnp.concatenate([g, o, core_swap(g), core_swap(o)], axis=0)
        d_mixed.append(dot_t(whole_grad, w_out[0]).astype(bf16))
    partials, saved = [], []
    for m in micros:
        query, own_keys, own_values = projections[m]
        keys, mixed, d_scores, kept, sent = call(
            backward_kernel,
            "backward",
            [("s", decoder)]
            + [("v", v) for v in (memories[m], others[m], mates[m], core_swap(others[m]))]
            + [("a", w_qkv)]
            + [("v", v) for v in (query, own_keys, own_values, d_mixed[m])],
            [(narrow, bf16)] * 3 + pair,
            [
                pltpu.VMEM(whole, bf16),
                pltpu.VMEM((2,) + w_qkv.shape[2:], bf16),
                pltpu.VMEM(narrow, bf16),
                pltpu.VMEM(narrow, bf16),
                pltpu.VMEM(narrow, bf16),
                pltpu.SemaphoreType.DMA((2,)),
            ],
            2.5,
        )
        rest = (keys, mixed, d_scores)
        if m == 0:
            kept, sent, others[1] = together(kept, sent, others[1])
        else:
            kept, sent, rest, saved[0] = together(kept, sent, rest, saved[0])
        partials.append((kept, sent))
        saved.append(rest)
    first = sum_cores(*partials[0])
    first, saved = together(first, saved)

    rests = []
    for m in micros:
        made = call(
            rest_kernel,
            "rest",
            [("s", decoder)]
            + [("v", v) for v in saved[m]]
            + [("a", w_qkv), ("a", w_out)]
            + [("v", v) for v in partials[m]],
            pair * 2,
            [
                pltpu.VMEM(w_qkv.shape[2:], bf16),
                pltpu.VMEM(w_out.shape[1:], bf16),
                pltpu.VMEM(narrow, bf16),
                pltpu.SemaphoreType.DMA((2,)),
            ],
            1.2,
        )
        rests += [sum_cores(*made[:2]), sum_cores(*made[2:])]
    total = [sum_chips(*first), scatter_sum(*partials[1])]
    total = jnp.concatenate(total, axis=1)
    quarter, eighth = rows // NX, rows // (NX * NY)

    def quarter_of(v, x):
        return lax.dynamic_slice_in_dim(v, x * quarter, quarter, axis=0)

    def eighth_of(v, y):
        return lax.dynamic_slice_in_dim(v, y * eighth, eighth, axis=0)

    got = move(quarter_of(enc_last, x_id ^ 3), x_perm(3, (2, 3)))
    last = eighth_of(jnp.where(is_decoder, quarter_of(enc_last, x_id), got), y_id)
    total = jnp.where(is_decoder, total, 0.0)
    wire = total.astype(bf16)
    total, last, rests = together(total, last, rests)
    rests = [sum_chips(*v) for v in rests]

    last = [last[:, : last.shape[1] // 2], last[:, last.shape[1] // 2 :]]
    total = quarter_of(total, x_id)
    for k in (1, 2, 3):
        got = move(quarter_of(wire, x_id ^ k), x_perm(k, (2, 3)))
        total = total + got.astype(jnp.float32)
    got = jump(eighth_of(total, y_id ^ 1).astype(jnp.bfloat16), Y_NEXT)
    total = eighth_of(total, y_id) + got.astype(jnp.float32)
    for k in (4, 2, 1):
        if k == 1:
            total, rests[0] = together(total, rests[0])
        wire = total.astype(jnp.bfloat16)
        total = wire.astype(jnp.float32) + move(wire, z_swap(k)).astype(jnp.float32)
    total, rests[1] = together(total, rests[1])
    total = [total[:, : total.shape[1] // 2], total[:, total.shape[1] // 2 :]]
    out = []
    for m in micros:
        inverse = normalize(last[m], final_gain)[1]
        out.append(norm_back(last[m], inverse, total[m] * final_gain, 0.0).astype(jnp.bfloat16))
    out = jnp.concatenate(out, axis=1)
    got, first = jump(out, Y_BACK), jump(out, Y_PAIR)
    out = jnp.where(
        y_id == 0, jnp.concatenate([first, got], axis=0), jnp.concatenate([got, out], axis=0)
    )
    out, rests[2] = together(out, rests[2])
    section_out, grad_in = [], []
    for m in micros:
        d_normed, summed = rests[2 * m], rests[2 * m + 1]
        base = grads[m].astype(jnp.float32)
        base = norm_back(inputs[m], norms[m][1], d_normed * gain, base)
        grad_in.append(base.astype(jnp.bfloat16))
        section_out.append((inputs[m].astype(jnp.float32) + summed).astype(jnp.bfloat16))
    parts = [out] + [move(out, x_perm(k, range(NX))) for k in (1, 2, 3)]
    odd, high = (x_id & 1) == 1, (x_id & 2) == 2
    parts = [jnp.where(odd, parts[j ^ 1], parts[j]) for j in range(NX)]
    parts = [jnp.where(high, parts[j ^ 2], parts[j]) for j in range(NX)]
    out = jnp.concatenate(parts, axis=0)
    memory_grad_out = [out[:, : out.shape[1] // 2], out[:, out.shape[1] // 2 :]]

    return tuple(
        jnp.stack(v, axis=1)[None] for v in (section_out, grad_in, memory_grad_out)
    )


def solution(mesh):
    in_specs = (
        P("section", "tp", None, None),
        P("section", "tp", None, None),
        P("section", None, None, "tp"),
        P("section", "tp", None),
        P("section", None),
        P(),
    )
    out_specs = (
        P("section", "tp", None, None),
        P("section", "tp", None, None),
        P("section", "tp", None, None),
    )
    return jax.shard_map(local, mesh=mesh, in_specs=in_specs, out_specs=out_specs, check_vma=False)
```
